32 devices in a mesh: member: 4 (over x, core), tile: 8 (over z, y).
Axes of the slice: x: 2, y: 2, z: 4, core: 2. Of those that a mesh axis runs over, the one named last changes fastest.
Arguments:
- noisy_state: float32 [4, 4, 512, 128], P('member', None, 'tile'), may hold values from -8 to 8
- churn_noise: float32 [4, 4, 512, 128], P('member', None, 'tile'), may hold values from -6 to 6
- coarse_cond: bfloat16 [16, 512, 128], P('member', 'tile'), may hold values from -6 to 6
- land_mask: int32 [512, 128], P('tile'), may hold values 0 or 1
- step_index: int32 [1], replicated, may hold values from 9 to 16
- owners: int32 [8, 16, 1], replicated, may hold values from 0 to 7; in each aligned block of 16 rows (0 to 15, 16 to 31, ..., all dimensions but the last counted through in order) at most 2 rows name the same one
- patch_rows: int32 [8, 16], replicated, may hold values from 0 to 32
- patch_cols: int32 [8, 16], replicated, may hold values from 0 to 96
- w_in: bfloat16 [128, 20], replicated, may hold values from -1.25 to 1.25
- b_in: float32 [128], replicated, may hold values from -3 to 3
- w_emb: float32 [128, 128], replicated, may hold values from -0.5 to 0.5
- w_conv: bfloat16 [9, 128, 128], replicated, may hold values from -0.1875 to 0.1875
- gn_gain: float32 [128], replicated, may hold values from 0.5 to 1.5
- gn_bias: float32 [128], replicated, may hold values from -3 to 3
- w_out: bfloat16 [4, 128], replicated, may hold values from -0.5 to 0.5
- b_out: float32 [4], replicated, may hold values from -3 to 3
Outputs:
- next_state: float32 [4, 4, 512, 128], P('member', None, 'tile')
The draws below stay inside these ranges and needn't reach their ends.
Inputs may be any that keep to these rules, and one draw needn't show every extreme that they name: `owners`: at most 2 patches of one worker's list lie on one owner tile, and some worker has exactly 2 on one; every tile owns a patch of some list.
All inputs are finite; a program needn't handle non-finite values. No bound on the sum of `land_mask` on one device may be relied on, other than what follows from the above.
Results may differ from the reference program's by a relative error of at most 0.00041.
Values may be sent and summed in bfloat16 or wider, within the bound.
A program may use at most 64 MiB of HBM per device.

```python
import math
import jax
import jax.numpy as jnp
import numpy as np
from jax import lax

CH = 128
C_COND = 16
V = 4
C_IN = 20
PH = 32
PW = 32
TH = 64
TW = 128
SLOTS = 16
CAP = 2
NSTEPS = 18
MEMBERS = 4
GH = 512
N_TILE = 8


def with_ends(values, own_key, smallest, high):
    longest = values.shape.index(max(values.shape))
    spots = []
    for shift in (0, 1):
        where = [jax.random.randint(jax.random.fold_in(own_key, axis), (), 0, length) for axis, length in enumerate(values.shape)]
        where[longest] = (where[longest] + shift) % values.shape[longest]
        spots.append(tuple(where))
    return values.at[spots[0]].set(smallest).at[spots[1]].set(high)


def steps_of(rng, dims, shards, least, top_value):
    def one(dim, blocks):
        heights = jax.random.uniform(jax.random.fold_in(jax.random.fold_in(rng, 6), dim), (blocks,), jnp.float32, least / len(shards), top_value / len(shards))
        return jnp.repeat(jnp.exp(heights), dims[dim] // blocks).reshape((-1,) + (1,) * (len(dims) - dim - 1))

    factor_of = one(*shards[0])
    for cut in shards[1:]:
        factor_of = factor_of * one(*cut)
    return factor_of


def deal_out(key, own, number, rows, amount, top, limit, skew):
    sequence = jax.random.permutation(key, amount)
    crowded, ordinary = portions_of(amount, rows * top, limit, skew, True), portions_of(amount, rows * top, limit, skew, False)
    places = jnp.arange(amount)

    def named(sizes, rotation):
        used = int((sizes > 0).sum())
        fixed = max(1, used // 4)
        passed = fixed + (places - fixed + rotation * (used - fixed)) % max(1, amount - fixed)
        return jnp.zeros((amount,), jnp.int32).at[sequence[jnp.where(places < fixed, places, passed)]].set(jnp.asarray(sizes, jnp.int32))

    sizes = jnp.where(number % 4 == 0, named(crowded, number // 4), named(ordinary, number - number // 4 - 1))
    mixed = jax.random.permutation(jax.random.fold_in(own, 3), amount)
    giver, receiver = mixed[0:amount // 2 * 2:2], mixed[1:amount // 2 * 2:2]
    slack = jnp.minimum(sizes[giver] - 1, limit - sizes[receiver]) // 2
    slack = jnp.where((giver == sequence[0]) | (receiver == sequence[0]) | (sizes[receiver] == 0), 0, jnp.maximum(slack, 0))
    passed = jax.random.randint(jax.random.fold_in(own, 4), (amount // 2,), 0, 1 << 20) % (slack + 1)
    sizes = sizes.at[giver].add(-passed).at[receiver].add(passed)
    labels = jnp.searchsorted(jnp.cumsum(sizes), jnp.arange(rows * top), side="right").astype(jnp.int32)
    table = labels.reshape(top, rows).T
    table = table[jax.random.permutation(jax.random.fold_in(own, 1), rows)]
    rotation = jax.random.randint(jax.random.fold_in(own, 2), (rows, 1), 0, top)
    return jnp.take_along_axis(table, (jnp.arange(top)[None, :] + rotation) % top, axis=1)


def portions_of(amount, total, reach, lean, full):
    weights = [(1 << 20) // math.isqrt(grade ** lean) + 1 for grade in range(1, amount + 1)]
    largest = reach if full else min(reach, max(-(-total // amount), total * weights[0] // sum(weights)))
    least = 1 if total - largest >= amount - 1 else 0
    given, rest = [largest] + [least] * (amount - 1), total - largest - least * (amount - 1)
    while rest > 0:
        free = [i for i in range(1, amount) if given[i] < largest] or [i for i in range(1, amount) if given[i] < reach]
        whole, left = sum([weights[i] for i in free]), rest
        for i in free:
            more = min(reach - given[i], max(1, left * weights[i] // whole), rest)
            given[i] = given[i] + more
            rest = rest - more
    return np.array(given)


def normal_values(rng, dims, spread, limit, cuts=(), kind=jnp.bfloat16):
    factor_of = steps_of(rng, dims, cuts, -0.22, 0.18) if cuts else 1.0
    result = jax.random.normal(rng, dims, jnp.float32) * spread * factor_of
    return jnp.minimum(jnp.maximum(result, -limit), limit).astype(kind)


def setup_inputs(seed: int = 0) -> dict:
    seeds = jax.random.split(jax.random.key(seed), 17)
    noisy_state = normal_values(seeds[0], (MEMBERS, V, GH, TW), 2.0, 8.0, ((0, 4), (2, 8)), jnp.float32)
    churn_noise = normal_values(seeds[1], (MEMBERS, V, GH, TW), 1.0, 6.0, ((0, 4), (2, 8)), jnp.float32)
    coarse_cond = normal_values(seeds[2], (C_COND, GH, TW), 1.0, 6.0, ((0, 4), (1, 8)))
    land_mask = with_ends((jax.random.randint(seeds[3], (GH, TW), 0, 4) < 3).astype(jnp.int32), jax.random.fold_in(seeds[3], 1), 0, 1)
    step_index = jax.random.randint(seeds[4], (1,), 9, NSTEPS - 1).astype(jnp.int32)
    owners_keys = jax.random.split(jax.random.fold_in(seeds[5], 1), N_TILE * SLOTS // SLOTS)
    owners_turns = jax.random.permutation(jax.random.fold_in(seeds[5], 3), N_TILE * SLOTS // SLOTS)
    owners = jax.vmap(lambda own, number: deal_out(jax.random.fold_in(seeds[5], 2), own, number, SLOTS, N_TILE, 1, CAP, 2))(owners_keys, owners_turns).reshape((N_TILE, SLOTS, 1))
    patch_rows = with_ends(jax.random.randint(seeds[6], (N_TILE, SLOTS), 0, TH - PH + 1), jax.random.fold_in(seeds[6], 1), 0, TH - PH).astype(jnp.int32)
    patch_cols = with_ends(jax.random.randint(seeds[7], (N_TILE, SLOTS), 0, TW - PW + 1), jax.random.fold_in(seeds[7], 1), 0, TW - PW).astype(jnp.int32)
    w_in = normal_values(seeds[8], (CH, C_IN), C_IN ** -0.5, 1.25)
    b_in = normal_values(seeds[9], (CH,), 0.5, 3.0, (), jnp.float32)
    w_emb = normal_values(seeds[10], (CH, CH), CH ** -0.5, 0.5, (), jnp.float32)
    w_conv = normal_values(seeds[11], (9, CH, CH), (9 * CH) ** -0.5, 0.1875)
    gn_gain = jnp.clip(jax.random.uniform(seeds[12], (CH,), jnp.float32, 0.5, 1.5), 0.5, 1.5)
    gn_bias = normal_values(seeds[13], (CH,), 0.5, 3.0, (), jnp.float32)
    w_out = normal_values(seeds[14], (V, CH), CH ** -0.5, 0.5)
    b_out = normal_values(seeds[15], (V,), 1.0, 3.0, (), jnp.float32)
    return {"noisy_state": noisy_state, "churn_noise": churn_noise, "coarse_cond": coarse_cond, "land_mask": land_mask, "step_index": step_index, "owners": owners, "patch_rows": patch_rows, "patch_cols": patch_cols, "w_in": w_in, "b_in": b_in, "w_emb": w_emb, "w_conv": w_conv, "gn_gain": gn_gain, "gn_bias": gn_bias, "w_out": w_out, "b_out": b_out}


SIGMA_DATA = 0.5
GAMMA = 0.25

def sigma_at(index_value):
    top_root = 800.0 ** (1.0 / 7.0)
    low_root = 0.002 ** (1.0 / 7.0)
    fraction = index_value.astype(jnp.float32) / (NSTEPS - 1)
    return (top_root + fraction * (low_root - top_root)) ** 7

def precondition(step_index, w_emb):
    sigma_now = sigma_at(step_index[0])
    sigma_next = sigma_at(step_index[0] + 1)
    sigma_hat = (1.0 + GAMMA) * sigma_now
    sigma_sq_sum = sigma_hat * sigma_hat + SIGMA_DATA * SIGMA_DATA
    scale_in = 1.0 / jnp.sqrt(sigma_sq_sum)
    scale_skip = SIGMA_DATA * SIGMA_DATA / sigma_sq_sum
    scale_out = SIGMA_DATA * sigma_hat / jnp.sqrt(sigma_sq_sum)
    churn_scale = jnp.sqrt(GAMMA * (2.0 + GAMMA)) * sigma_now
    noise_level = jnp.log(sigma_hat) / 4.0
    half_width = w_emb.shape[1] // 2
    frequency = jnp.exp(-jnp.log(10000.0) * jnp.arange(half_width, dtype=jnp.float32) / half_width)
    angles = 1000.0 * noise_level * frequency
    features = jnp.concatenate([jnp.cos(angles), jnp.sin(angles)])
    embedding = jnp.dot(w_emb, features, precision=lax.Precision.HIGHEST)
    return (sigma_hat, sigma_next, scale_in, scale_skip, scale_out, churn_scale, embedding)

def window_weights(length):
    position = jnp.arange(length, dtype=jnp.float32)
    return 0.3 + 0.7 * jnp.sin(jnp.pi * (position + 0.5) / length)

def blend_table():
    return (window_weights(PH)[:, None] * window_weights(PW)[None, :]).reshape(-1)

def denoiser(patch_data, net_params, embedding):
    w_in, b_in, w_conv, gn_gain, gn_bias, w_out, b_out = net_params
    pre_act = jnp.dot(w_in, patch_data, preferred_element_type=jnp.float32) + (b_in + embedding)[:, None]
    hidden = jax.nn.silu(pre_act).astype(jnp.bfloat16)
    cell_count = hidden.shape[1]
    padded = jnp.pad(hidden, ((0, 0), (PW + 1, PW + 1)))
    column = jnp.arange(cell_count) % PW
    left_ok = (column >= 1).astype(jnp.bfloat16)
    right_ok = (column <= PW - 2).astype(jnp.bfloat16)
    convolved = jnp.zeros((w_conv.shape[1], cell_count), jnp.float32)
    for row_step in (-1, 0, 1):
        for col_step in (-1, 0, 1):
            start_cell = PW + 1 + row_step * PW + col_step
            shifted = lax.slice_in_dim(padded, start_cell, start_cell + cell_count, axis=1)
            if col_step == -1:
                shifted = shifted * left_ok[None, :]
            if col_step == 1:
                shifted = shifted * right_ok[None, :]
            tap_index = (row_step + 1) * 3 + (col_step + 1)
            convolved = convolved + jnp.dot(w_conv[tap_index], shifted, preferred_element_type=jnp.float32)
    grouped = convolved.reshape(32, -1)
    group_mean = lax.optimization_barrier(jnp.mean(grouped, axis=1, keepdims=True))
    group_var = lax.optimization_barrier(jnp.mean((grouped - group_mean) ** 2, axis=1, keepdims=True))
    normed = ((grouped - group_mean) * lax.rsqrt(group_var + 1e-06)).reshape(convolved.shape)
    normed = normed * gn_gain[:, None] + gn_bias[:, None]
    residual = (hidden.astype(jnp.float32) + jax.nn.silu(normed)).astype(jnp.bfloat16)
    return jnp.dot(w_out, residual, preferred_element_type=jnp.float32) + b_out[:, None]

def extract_patches(inputs, row_list, col_list):
    channels = inputs.shape[0]
    zero_index = jnp.zeros((), jnp.int32)

    def one_patch(row_start, col_start):
        sliced = lax.dynamic_slice(inputs, (zero_index, row_start.astype(jnp.int32), col_start.astype(jnp.int32)), (channels, PH, PW))
        return sliced.reshape(channels, PH * PW)
    return jax.vmap(one_patch)(row_list, col_list)

def place_patches(running_total, blended, row_list, col_list):
    variables = blended.shape[1]
    zero_index = jnp.zeros((), jnp.int32)

    def add_one(slot_index, running):
        corner = (zero_index, row_list[slot_index].astype(jnp.int32), col_list[slot_index].astype(jnp.int32))
        current = lax.dynamic_slice(running, corner, (variables, PH, PW))
        return lax.dynamic_update_slice(running, current + blended[slot_index].reshape(variables, PH, PW), corner)
    return lax.fori_loop(0, blended.shape[0], add_one, running_total)

def coverage(row_list, col_list, live_mask, row_count, col_count):
    row_offset = (jnp.arange(row_count)[None, :] - row_list[:, None]).astype(jnp.float32)
    col_offset = (jnp.arange(col_count)[None, :] - col_list[:, None]).astype(jnp.float32)
    row_weight = (0.3 + 0.7 * jnp.sin(jnp.pi * (row_offset + 0.5) / PH)) * ((row_offset >= 0) & (row_offset < PH)).astype(jnp.float32)
    col_weight = (0.3 + 0.7 * jnp.sin(jnp.pi * (col_offset + 0.5) / PW)) * ((col_offset >= 0) & (col_offset < PW)).astype(jnp.float32)
    row_weight = row_weight * live_mask[:, None]
    return jnp.dot(row_weight.T, col_weight, precision=lax.Precision.HIGHEST)

def finish_step(x_hat, accumulated, weights, land_mask, constants):
    sigma_hat, sigma_next, scale_in, scale_skip, scale_out, churn_scale, embedding = constants
    land_value = land_mask.astype(jnp.float32)
    denoised = land_value * (weights * scale_skip * x_hat + scale_out * accumulated) / jnp.maximum(weights, 0.25)
    return x_hat + (sigma_next - sigma_hat) / sigma_hat * (x_hat - denoised)

def reference(noisy_state, churn_noise, coarse_cond, land_mask, step_index, owners, patch_rows, patch_cols, w_in, b_in, w_emb, w_conv, gn_gain, gn_bias, w_out, b_out):
    constants = precondition(step_index, w_emb)
    scale_in = constants[2]
    churn_scale = constants[5]
    embedding = constants[6]
    net_params = (w_in, b_in, w_conv, gn_gain, gn_bias, w_out, b_out)
    x_hat = noisy_state + churn_scale * churn_noise
    scaled = (scale_in * x_hat).astype(jnp.bfloat16)
    owner_flat = owners.reshape(-1).astype(jnp.int32)
    row_global = owner_flat * TH + patch_rows.reshape(-1).astype(jnp.int32)
    col_flat = patch_cols.reshape(-1).astype(jnp.int32)
    blend = blend_table()
    weights = coverage(row_global, col_flat, jnp.ones(row_global.shape, jnp.float32), GH, TW)
    results = []
    for member in range(MEMBERS):
        inputs = jnp.concatenate([coarse_cond, scaled[member]], axis=0)
        patches = extract_patches(inputs, row_global, col_flat)
        blended = lax.map(lambda patch_data: denoiser(patch_data, net_params, embedding), patches) * blend[None, None, :]
        accumulated = place_patches(jnp.zeros((V, GH, TW), jnp.float32), blended, row_global, col_flat)
        results.append(finish_step(x_hat[member], accumulated, weights, land_mask, constants))
    return jnp.stack(results)
```

```python
import functools

import jax
import jax.numpy as jnp
import numpy as np
from jax import lax
from jax.experimental import pallas as pl
from jax.experimental.pallas import tpu as pltpu
from jax.sharding import PartitionSpec as P

PH = 32
PW = 32
NSTEPS = 18


SIGMA_DATA = 0.5
GAMMA = 0.25


def sigma_at(index_value):
    top_root = 800.0 ** (1.0 / 7.0)
    low_root = 0.002 ** (1.0 / 7.0)
    fraction = index_value.astype(jnp.float32) / (NSTEPS - 1)
    return (top_root + fraction * (low_root - top_root)) ** 7


def precondition(step_index, w_emb):
    sigma_now = sigma_at(step_index[0])
    sigma_next = sigma_at(step_index[0] + 1)
    sigma_hat = (1.0 + GAMMA) * sigma_now
    sigma_sq_sum = sigma_hat * sigma_hat + SIGMA_DATA * SIGMA_DATA
    scale_in = 1.0 / jnp.sqrt(sigma_sq_sum)
    scale_skip = SIGMA_DATA * SIGMA_DATA / sigma_sq_sum
    scale_out = SIGMA_DATA * sigma_hat / jnp.sqrt(sigma_sq_sum)
    churn_scale = jnp.sqrt(GAMMA * (2.0 + GAMMA)) * sigma_now
    noise_level = jnp.log(sigma_hat) / 4.0
    half_width = w_emb.shape[1] // 2
    frequency = jnp.exp(-jnp.log(10000.0) * jnp.arange(half_width, dtype=jnp.float32) / half_width)
    angles = 1000.0 * noise_level * frequency
    features = jnp.concatenate([jnp.cos(angles), jnp.sin(angles)])
    embedding = jnp.dot(w_emb, features, precision=lax.Precision.HIGHEST)
    return (sigma_hat, sigma_next, scale_in, scale_skip, scale_out, churn_scale, embedding)


def window_weights(length):
    position = np.arange(length, dtype=np.float64)
    return 0.3 + 0.7 * np.sin(np.pi * (position + 0.5) / length)


def gather_kernel(axis_size, part_ref, whole_ref, send_sem, recv_sem, local_sem):
    me = lax.axis_index("member")
    depth = part_ref.shape[0]
    barrier = pltpu.get_barrier_semaphore()
    for step in range(1, axis_size):
        pl.semaphore_signal(
            barrier,
            inc=1,
            device_id={"member": lax.rem(me + step, axis_size)},
            device_id_type=pl.DeviceIdType.MESH,
        )
    pl.semaphore_wait(barrier, axis_size - 1)
    own = whole_ref.at[pl.ds(me * depth, depth)]
    copies = []
    for step in range(1, axis_size):
        copy = pltpu.make_async_remote_copy(
            src_ref=part_ref,
            dst_ref=own,
            send_sem=send_sem.at[step - 1],
            recv_sem=recv_sem.at[step - 1],
            device_id={"member": lax.rem(me + step, axis_size)},
            device_id_type=pl.DeviceIdType.MESH,
        )
        copy.start()
        copies.append(copy)
    local = pltpu.make_async_copy(part_ref, own, local_sem)
    local.start()
    local.wait()
    for copy in copies:
        copy.wait()


def gather_members(part, axis_size):
    shape = (part.shape[0] * axis_size,) + part.shape[1:]
    return pl.pallas_call(
        functools.partial(gather_kernel, axis_size),
        out_shape=jax.ShapeDtypeStruct(shape, part.dtype),
        in_specs=[pl.BlockSpec(memory_space=pltpu.VMEM)],
        out_specs=pl.BlockSpec(memory_space=pltpu.VMEM),
        scratch_shapes=[
            pltpu.SemaphoreType.DMA((axis_size - 1,)),
            pltpu.SemaphoreType.DMA((axis_size - 1,)),
            pltpu.SemaphoreType.DMA,
        ],
        compiler_params=pltpu.CompilerParams(collective_id=0, has_side_effects=True),
    )(part)


LEAD = 8
K_IN = 32


def silu(value):
    half = 0.5 * value
    return half + half * jnp.tanh(half)


def group_sum(value):
    lane = lax.broadcasted_iota(jnp.int32, value.shape, 1)
    width = value.shape[1]
    pair = value + jnp.where(
        lane % 2 == 0, pltpu.roll(value, width - 1, 1), pltpu.roll(value, 1, 1)
    )
    return pair + jnp.where(
        lane % 4 < 2, pltpu.roll(pair, width - 2, 1), pltpu.roll(pair, 2, 1)
    )


def tile_kernel(
    scalars,
    owners,
    patch_rows,
    patch_cols,
    b_out,
    cond,
    noisy,
    churn,
    land,
    bias_in,
    w_in,
    w_conv,
    gn_gain,
    gn_bias,
    w_out,
    blend_cells,
    blend_lanes,
    out,
    row_list,
    col_list,
    inputs,
    w_square,
    hidden,
    total,
    taps,
    w_pairs,
    conv,
    weights,
    flat,
):
    self_tile = lax.axis_index("tile")
    channels = w_conv.shape[1]
    variables, tile_rows, tile_cols = noisy.shape
    cond_channels = cond.shape[0]
    scale_in = scalars[0]
    churn_scale = scalars[1]
    scale_skip = scalars[2]
    scale_out = scalars[3]
    step_ratio = scalars[4]

    def note_patch(index, count):
        row_list[count] = patch_rows[index]
        col_list[count] = patch_cols[index]
        return count + (owners[index] == self_tile).astype(jnp.int32)

    count = lax.fori_loop(0, owners.shape[0], note_patch, jnp.int32(0), unroll=8)

    for channel in range(cond_channels):
        inputs[channel * tile_rows : (channel + 1) * tile_rows, :] = cond[channel].astype(
            jnp.float32
        )
    for variable in range(variables):
        start = (cond_channels + variable) * tile_rows
        x_hat = noisy[variable] + churn_scale * churn[variable]
        inputs[start : start + tile_rows, :] = (
            (scale_in * x_hat).astype(jnp.bfloat16).astype(jnp.float32)
        )
    used = cond_channels + variables
    inputs[used * tile_rows :, :] = jnp.zeros(
        ((K_IN - used) * tile_rows, tile_cols), jnp.float32
    )
    w_square[...] = jnp.zeros_like(w_square)
    w_square[:, 0:used] = w_in[...].astype(jnp.float32)
    w_first = w_square[...].T[0:K_IN].astype(jnp.bfloat16)
    bias = bias_in[...]

    def hidden_row(row, carry):
        cells = inputs[pl.ds(row, K_IN, stride=tile_rows), :].T.astype(jnp.bfloat16)
        pre_act = jnp.dot(cells, w_first, preferred_element_type=jnp.float32) + bias
        hidden[row, LEAD : LEAD + tile_cols, :] = (
            silu(pre_act).astype(jnp.bfloat16).astype(jnp.float32)
        )
        total[row] = jnp.zeros((tile_cols, channels), jnp.float32)
        return carry

    lax.fori_loop(0, tile_rows, hidden_row, 0, unroll=4)

    zero_block = jnp.zeros((channels, channels), jnp.bfloat16)
    for col in range(3):
        tap = [w_conv[3 * a + col].astype(jnp.float32).T.astype(jnp.bfloat16) for a in range(3)]
        blocks = (
            ((tap[0], zero_block), (tap[1], tap[0])),
            ((tap[2], tap[1]), (zero_block, tap[2])),
        )
        for half in range(2):
            start = (2 * col + half) * 2 * channels
            for k in range(2):
                for o in range(2):
                    w_pairs[
                        start + k * channels : start + (k + 1) * channels,
                        o * channels : (o + 1) * channels,
                    ] = blocks[half][k][o]
        taps[col, 0, :, 0:channels] = jnp.zeros((PW, channels), jnp.bfloat16)
        taps[col, PH // 2, :, channels : 2 * channels] = jnp.zeros((PW, channels), jnp.bfloat16)
    weights[...] = jnp.zeros_like(weights)

    gain = jnp.concatenate([gn_gain[...], gn_gain[...]], axis=1)
    shift = jnp.concatenate([gn_bias[...], gn_bias[...]], axis=1)
    lanes = blend_lanes[...]
    cell_count = PH * PW
    inverse = 1.0 / (4 * cell_count)
    position = lax.broadcasted_iota(jnp.int32, (PW, channels), 0)

    def spread(value):
        value = group_sum(value[:, 0:channels] + value[:, channels : 2 * channels])
        return jnp.concatenate([value, value], axis=1)

    def one_patch(slot, carry):
        row_start = row_list[slot]
        col_start = col_list[slot]
        weights[pl.ds(row_start, PH), :] += pltpu.roll(lanes, col_start, 1)
        for i in range(PH):
            pair = (i + 1) // 2
            lane = 0 if i % 2 else channels
            for col in range(3):
                piece = hidden[row_start + i, pl.ds(col_start + (LEAD - 1 + col), PW), :]
                if col == 0:
                    piece = jnp.where(position == 0, 0.0, piece)
                if col == 2:
                    piece = jnp.where(position == PW - 1, 0.0, piece)
                taps[col, pair, :, lane : lane + channels] = piece.astype(jnp.bfloat16)
        half_cells = cell_count // 2
        left = jnp.concatenate(
            [
                taps[col, half : half + PH // 2].reshape(half_cells, 2 * channels)
                for col in range(3)
                for half in range(2)
            ],
            axis=1,
        )
        convolved = jnp.dot(left, w_pairs[...], preferred_element_type=jnp.float32)
        conv[...] = convolved
        mean = spread(jnp.sum(convolved, axis=0, keepdims=True)) * inverse
        centred = conv[...] - mean
        var = spread(jnp.sum(centred * centred, axis=0, keepdims=True)) * inverse
        scale = lax.rsqrt(var + 1e-06) * gain
        for t in range(PH // 2):
            normed = (conv[t * PW : (t + 1) * PW, :] - mean) * scale + shift
            active = silu(normed)
            for o in range(2):
                i = 2 * t + o
                own = hidden[row_start + i, pl.ds(col_start + LEAD, PW), :]
                residual = (
                    (own + active[:, o * channels : (o + 1) * channels])
                    .astype(jnp.bfloat16)
                    .astype(jnp.float32)
                )
                total[row_start + i, pl.ds(col_start, PW), :] += residual * blend_cells[i]
        return carry

    lax.fori_loop(0, count, one_patch, 0)

    w_square[0:16, :] = jnp.zeros((16, channels), jnp.float32)
    w_square[0:variables, :] = w_out[...].astype(jnp.float32)
    w_last = w_square[0:16, :].astype(jnp.bfloat16)
    w_last = jnp.concatenate([w_last, w_last], axis=1)

    def project(block, carry):
        value = total[pl.ds(block * 8, 8)].reshape(8 * tile_cols, channels)
        high = value.astype(jnp.bfloat16)
        low = (value - high.astype(jnp.float32)).astype(jnp.bfloat16)
        result = lax.dot_general(
            w_last,
            jnp.concatenate([high, low], axis=1),
            (((1,), (1,)), ((), ())),
            preferred_element_type=jnp.float32,
        )
        for j in range(8):
            flat[pl.ds(pl.multiple_of(block * 64, 64) + j * 8, 8), :] = result[
                0:8, j * tile_cols : (j + 1) * tile_cols
            ]
        return carry

    lax.fori_loop(0, tile_rows // 8, project, 0)

    cover = weights[...]
    land_value = land[...].astype(jnp.float32) / jnp.maximum(cover, 0.25)
    for variable in range(variables):
        x_hat = noisy[variable] + churn_scale * churn[variable]
        accumulated = flat[pl.ds(variable, tile_rows, stride=8), :] + b_out[variable] * cover
        denoised = land_value * (cover * scale_skip * x_hat + scale_out * accumulated)
        out[variable] = x_hat + step_ratio * (x_hat - denoised)


def body(
    noisy_state,
    churn_noise,
    coarse_cond,
    land_mask,
    step_index,
    owners,
    patch_rows,
    patch_cols,
    w_in,
    b_in,
    w_emb,
    w_conv,
    gn_gain,
    gn_bias,
    w_out,
    b_out,
):
    sigma_hat, sigma_next, scale_in, scale_skip, scale_out, churn_scale, embedding = precondition(
        step_index, w_emb
    )
    step_ratio = (sigma_next - sigma_hat) / sigma_hat
    zero = jnp.zeros_like(scale_in)
    scalars = jnp.stack(
        [scale_in, churn_scale, scale_skip, scale_out, step_ratio, zero, zero, zero]
    )
    cond = gather_members(coarse_cond, lax.axis_size("member"))
    channels = w_conv.shape[1]
    variables, tile_rows, tile_cols = noisy_state.shape[1:]
    slots = owners.size
    blend = window_weights(PH)[:, None] * window_weights(PW)[None, :]
    blend_cells = jnp.asarray(
        np.broadcast_to(blend[:, :, None], (PH, PW, channels)).astype(np.float32)
    )
    blend_lanes = jnp.asarray(
        np.pad(blend, ((0, 0), (0, tile_cols - PW))).astype(np.float32)
    )
    smem = pl.BlockSpec(memory_space=pltpu.SMEM)
    vmem = pl.BlockSpec(memory_space=pltpu.VMEM)
    f32 = jnp.float32
    result = pl.pallas_call(
        tile_kernel,
        out_shape=jax.ShapeDtypeStruct((variables, tile_rows, tile_cols), f32),
        in_specs=[smem] * 5 + [vmem] * 12,
        out_specs=vmem,
        scratch_shapes=[
            pltpu.SMEM((slots + 1,), jnp.int32),
            pltpu.SMEM((slots + 1,), jnp.int32),
            pltpu.VMEM((K_IN * tile_rows, tile_cols), f32),
            pltpu.VMEM((channels, channels), f32),
            pltpu.VMEM((tile_rows, tile_cols + 2 * LEAD, channels), f32),
            pltpu.VMEM((tile_rows, tile_cols, channels), f32),
            pltpu.VMEM((3, PH // 2 + 1, PW, 2 * channels), jnp.bfloat16),
            pltpu.VMEM((12 * channels, 2 * channels), jnp.bfloat16),
            pltpu.VMEM((PH * PW // 2, 2 * channels), f32),
            pltpu.VMEM((tile_rows, tile_cols), f32),
            pltpu.VMEM((8 * tile_rows, tile_cols), f32),
        ],
        compiler_params=pltpu.CompilerParams(vmem_limit_bytes=40 * 1024 * 1024),
    )(
        scalars,
        owners.reshape(-1),
        patch_rows.reshape(-1),
        patch_cols.reshape(-1),
        b_out,
        cond,
        noisy_state[0],
        churn_noise[0],
        land_mask,
        (b_in + embedding)[None, :],
        w_in,
        w_conv,
        gn_gain[None, :],
        gn_bias[None, :],
        w_out,
        blend_cells,
        blend_lanes,
    )
    return result[None]


def solution(mesh):
    return jax.shard_map(
        body,
        mesh=mesh,
        in_specs=(
            P("member", None, "tile", None),
            P("member", None, "tile", None),
            P("member", "tile", None),
            P("tile", None),
            P(),
            P(),
            P(),
            P(),
            P(),
            P(),
            P(),
            P(),
            P(),
            P(),
            P(),
            P(),
        ),
        out_specs=P("member", None, "tile", None),
        check_vma=False,
    )
```

```python
import functools

import jax
import jax.numpy as jnp
import numpy as np
from jax import lax
from jax.experimental import pallas as pl
from jax.experimental.pallas import tpu as pltpu
from jax.sharding import PartitionSpec as P

PH = 32
PW = 32
NSTEPS = 18


SIGMA_DATA = 0.5
GAMMA = 0.25


def noise_plan(half_width):
    index = np.arange(NSTEPS, dtype=np.float64)
    top_root = 800.0 ** (1.0 / 7.0)
    low_root = 0.002 ** (1.0 / 7.0)

    def sigma_at(position):
        return (top_root + position / (NSTEPS - 1) * (low_root - top_root)) ** 7

    sigma_now = sigma_at(index)
    sigma_next = sigma_at(index + 1)
    sigma_hat = (1.0 + GAMMA) * sigma_now
    sigma_sq_sum = sigma_hat * sigma_hat + SIGMA_DATA * SIGMA_DATA
    columns = [
        1.0 / np.sqrt(sigma_sq_sum),
        np.sqrt(GAMMA * (2.0 + GAMMA)) * sigma_now,
        SIGMA_DATA * SIGMA_DATA / sigma_sq_sum,
        SIGMA_DATA * sigma_hat / np.sqrt(sigma_sq_sum),
        (sigma_next - sigma_hat) / sigma_hat,
    ]
    columns += [np.zeros_like(index)] * (8 - len(columns))
    frequency = np.exp(-np.log(10000.0) * np.arange(half_width) / half_width)
    angles = 250.0 * np.log(sigma_hat)[:, None] * frequency[None, :]
    features = np.concatenate([np.cos(angles), np.sin(angles)], axis=1)
    return np.stack(columns, axis=1).reshape(-1).astype(np.float32), features.astype(np.float32)


def window_weights(length):
    position = np.arange(length, dtype=np.float64)
    return 0.3 + 0.7 * np.sin(np.pi * (position + 0.5) / length)


def gather_kernel(axis_size, part_ref, whole_ref, send_sem, recv_sem, local_sem):
    me = lax.axis_index("member")
    depth = part_ref.shape[0]
    barrier = pltpu.get_barrier_semaphore()
    for step in range(1, axis_size):
        pl.semaphore_signal(
            barrier,
            inc=1,
            device_id={"member": lax.rem(me + step, axis_size)},
            device_id_type=pl.DeviceIdType.MESH,
        )
    pl.semaphore_wait(barrier, axis_size - 1)
    own = whole_ref.at[pl.ds(me * depth, depth)]
    copies = []
    for step in range(1, axis_size):
        copy = pltpu.make_async_remote_copy(
            src_ref=part_ref,
            dst_ref=own,
            send_sem=send_sem.at[step - 1],
            recv_sem=recv_sem.at[step - 1],
            device_id={"member": lax.rem(me + step, axis_size)},
            device_id_type=pl.DeviceIdType.MESH,
        )
        copy.start()
        copies.append(copy)
    local = pltpu.make_async_copy(part_ref, own, local_sem)
    local.start()
    local.wait()
    for copy in copies:
        copy.wait()


def gather_members(part, axis_size):
    shape = (part.shape[0] * axis_size,) + part.shape[1:]
    return pl.pallas_call(
        functools.partial(gather_kernel, axis_size),
        out_shape=jax.ShapeDtypeStruct(shape, part.dtype),
        in_specs=[pl.BlockSpec(memory_space=pltpu.HBM)],
        out_specs=pl.BlockSpec(memory_space=pltpu.HBM),
        scratch_shapes=[
            pltpu.SemaphoreType.DMA((axis_size - 1,)),
            pltpu.SemaphoreType.DMA((axis_size - 1,)),
            pltpu.SemaphoreType.DMA,
        ],
        compiler_params=pltpu.CompilerParams(collective_id=0, has_side_effects=True),
    )(part)


LEAD = 8
K_IN = 32


def silu(value):
    half = 0.5 * value
    return half + half * jnp.tanh(half)


def group_sum(value):
    lane = lax.broadcasted_iota(jnp.int32, value.shape, 1)
    width = value.shape[1]
    pair = value + jnp.where(
        lane % 2 == 0, pltpu.roll(value, width - 1, 1), pltpu.roll(value, 1, 1)
    )
    return pair + jnp.where(
        lane % 4 < 2, pltpu.roll(pair, width - 2, 1), pltpu.roll(pair, 2, 1)
    )


def tile_kernel(
    step_index,
    plan_hbm,
    owners_hbm,
    patch_rows_hbm,
    patch_cols_hbm,
    b_out_hbm,
    w_conv_hbm,
    w_emb_hbm,
    features_hbm,
    b_in_hbm,
    noisy_hbm,
    churn_hbm,
    cond_hbm,
    w_in_hbm,
    land_hbm,
    gn_gain_hbm,
    gn_bias_hbm,
    blend_lanes_hbm,
    blend_cells_hbm,
    w_out_hbm,
    out,
    plan,
    owners,
    patch_rows,
    patch_cols,
    b_out,
    w_conv,
    w_emb,
    features,
    b_in,
    noisy,
    churn,
    cond,
    w_in,
    land,
    gn_gain,
    gn_bias,
    blend_lanes,
    blend_cells,
    w_out,
    operand_sem,
    row_list,
    col_list,
    inputs,
    w_square,
    hidden,
    total,
    taps,
    w_pairs,
    conv,
    weights,
    flat,
):
    pairs = (
        (plan_hbm, plan),
        (owners_hbm, owners),
        (patch_rows_hbm, patch_rows),
        (patch_cols_hbm, patch_cols),
        (b_out_hbm, b_out),
        (w_conv_hbm, w_conv),
        (w_emb_hbm, w_emb),
        (features_hbm, features),
        (b_in_hbm, b_in),
        (noisy_hbm, noisy),
        (churn_hbm, churn),
        (cond_hbm, cond),
        (w_in_hbm, w_in),
        (land_hbm, land),
        (gn_gain_hbm, gn_gain),
        (gn_bias_hbm, gn_bias),
        (blend_lanes_hbm, blend_lanes),
        (blend_cells_hbm, blend_cells),
        (w_out_hbm, w_out),
    )
    copies = [
        pltpu.make_async_copy(source, target, operand_sem.at[index])
        for index, (source, target) in enumerate(pairs)
    ]
    for copy in copies:
        copy.start()
    self_tile = lax.axis_index("tile")
    channels = w_conv.shape[1]
    variables, tile_rows, tile_cols = noisy.shape
    cond_channels = cond.shape[0]

    def clear_row(row, carry):
        total[row] = jnp.zeros((tile_cols, channels), jnp.float32)
        return carry

    lax.fori_loop(0, tile_rows, clear_row, 0, unroll=4)
    for copy in copies:
        copy.wait()
    zero_block = jnp.zeros((channels, channels), jnp.bfloat16)
    for col in range(3):
        tap = [w_conv[3 * a + col].astype(jnp.float32).T.astype(jnp.bfloat16) for a in range(3)]
        blocks = (
            ((tap[0], zero_block), (tap[1], tap[0])),
            ((tap[2], tap[1]), (zero_block, tap[2])),
        )
        for half in range(2):
            start = (2 * col + half) * 2 * channels
            for k in range(2):
                for o in range(2):
                    w_pairs[
                        start + k * channels : start + (k + 1) * channels,
                        o * channels : (o + 1) * channels,
                    ] = blocks[half][k][o]
        taps[col, 0, :, 0:channels] = jnp.zeros((PW, channels), jnp.bfloat16)
        taps[col, PH // 2, :, channels : 2 * channels] = jnp.zeros((PW, channels), jnp.bfloat16)
    weights[...] = jnp.zeros_like(weights)
    step = step_index[0]
    scale_in = plan[8 * step]
    churn_scale = plan[8 * step + 1]
    scale_skip = plan[8 * step + 2]
    scale_out = plan[8 * step + 3]
    step_ratio = plan[8 * step + 4]
    feature = jnp.broadcast_to(features[pl.ds(step, 1), :], (8, features.shape[1]))
    embedding = lax.dot_general(
        feature,
        w_emb[...],
        (((1,), (1,)), ((), ())),
        precision=lax.Precision.HIGHEST,
        preferred_element_type=jnp.float32,
    )
    bias = b_in[...] + embedding[0:1]
    slots = patch_rows.shape[1]

    def note_patch(index, count):
        for slot in range(slots):
            row_list[count] = patch_rows[index, slot]
            col_list[count] = patch_cols[index, slot]
            count = count + (owners[index, 0, slot] == self_tile).astype(jnp.int32)
        return count

    count = lax.fori_loop(0, patch_rows.shape[0], note_patch, jnp.int32(0))

    for channel in range(cond_channels):
        inputs[channel * tile_rows : (channel + 1) * tile_rows, :] = cond[channel].astype(
            jnp.float32
        )
    for variable in range(variables):
        start = (cond_channels + variable) * tile_rows
        x_hat = noisy[variable] + churn_scale * churn[variable]
        inputs[start : start + tile_rows, :] = (
            (scale_in * x_hat).astype(jnp.bfloat16).astype(jnp.float32)
        )
    used = cond_channels + variables
    inputs[used * tile_rows :, :] = jnp.zeros(
        ((K_IN - used) * tile_rows, tile_cols), jnp.float32
    )
    w_square[...] = jnp.zeros_like(w_square)
    w_square[0:used, :] = w_in[...].astype(jnp.float32)
    w_first = w_square[0:K_IN].astype(jnp.bfloat16)

    def hidden_row(row, carry):
        cells = inputs[pl.ds(row, K_IN, stride=tile_rows), :].T.astype(jnp.bfloat16)
        pre_act = jnp.dot(cells, w_first, preferred_element_type=jnp.float32) + bias
        hidden[row, LEAD : LEAD + tile_cols, :] = (
            silu(pre_act).astype(jnp.bfloat16).astype(jnp.float32)
        )
        return carry

    lax.fori_loop(0, tile_rows, hidden_row, 0, unroll=4)

    gain = jnp.concatenate([gn_gain[...], gn_gain[...]], axis=1)
    shift = jnp.concatenate([gn_bias[...], gn_bias[...]], axis=1)
    lanes = blend_lanes[...]
    cell_count = PH * PW
    inverse = 1.0 / (4 * cell_count)
    position = lax.broadcasted_iota(jnp.int32, (PW, channels), 0)

    def spread(value):
        value = group_sum(value[:, 0:channels] + value[:, channels : 2 * channels])
        return jnp.concatenate([value, value], axis=1)

    def one_patch(slot, carry):
        row_start = row_list[slot]
        col_start = col_list[slot]
        weights[pl.ds(row_start, PH), :] += pltpu.roll(lanes, col_start, 1)
        for i in range(PH):
            pair = (i + 1) // 2
            lane = 0 if i % 2 else channels
            for col in range(3):
                piece = hidden[row_start + i, pl.ds(col_start + (LEAD - 1 + col), PW), :]
                if col == 0:
                    piece = jnp.where(position == 0, 0.0, piece)
                if col == 2:
                    piece = jnp.where(position == PW - 1, 0.0, piece)
                taps[col, pair, :, lane : lane + channels] = piece.astype(jnp.bfloat16)
        half_cells = cell_count // 2
        left = jnp.concatenate(
            [
                taps[col, half : half + PH // 2].reshape(half_cells, 2 * channels)
                for col in range(3)
                for half in range(2)
            ],
            axis=1,
        )
        convolved = jnp.dot(left, w_pairs[...], preferred_element_type=jnp.float32)
        conv[...] = convolved
        mean = spread(jnp.sum(convolved, axis=0, keepdims=True)) * inverse
        centred = conv[...] - mean
        var = spread(jnp.sum(centred * centred, axis=0, keepdims=True)) * inverse
        scale = lax.rsqrt(var + 1e-06) * gain
        for t in range(PH // 2):
            normed = (conv[t * PW : (t + 1) * PW, :] - mean) * scale + shift
            active = silu(normed)
            for o in range(2):
                i = 2 * t + o
                own = hidden[row_start + i, pl.ds(col_start + LEAD, PW), :]
                residual = (
                    (own + active[:, o * channels : (o + 1) * channels])
                    .astype(jnp.bfloat16)
                    .astype(jnp.float32)
                )
                total[row_start + i, pl.ds(col_start, PW), :] += residual * blend_cells[i]
        return carry

    lax.fori_loop(0, count, one_patch, 0)

    w_square[0:16, :] = jnp.zeros((16, channels), jnp.float32)
    w_square[0:variables, :] = w_out[...].astype(jnp.float32)
    w_last = w_square[0:16, :].astype(jnp.bfloat16)
    w_last = jnp.concatenate([w_last, w_last], axis=1)

    def project(block, carry):
        value = total[pl.ds(block * 8, 8)].reshape(8 * tile_cols, channels)
        high = value.astype(jnp.bfloat16)
        low = (value - high.astype(jnp.float32)).astype(jnp.bfloat16)
        result = lax.dot_general(
            w_last,
            jnp.concatenate([high, low], axis=1),
            (((1,), (1,)), ((), ())),
            preferred_element_type=jnp.float32,
        )
        for j in range(8):
            flat[pl.ds(pl.multiple_of(block * 64, 64) + j * 8, 8), :] = result[
                0:8, j * tile_cols : (j + 1) * tile_cols
            ]
        return carry

    lax.fori_loop(0, tile_rows // 8, project, 0)

    cover = weights[...]
    land_value = land[...].astype(jnp.float32) / jnp.maximum(cover, 0.25)
    for variable in range(variables):
        x_hat = noisy[variable] + churn_scale * churn[variable]
        accumulated = flat[pl.ds(variable, tile_rows, stride=8), :] + b_out[variable] * cover
        denoised = land_value * (cover * scale_skip * x_hat + scale_out * accumulated)
        out[variable] = x_hat + step_ratio * (x_hat - denoised)


def body(
    noisy_state,
    churn_noise,
    coarse_cond,
    land_mask,
    step_index,
    owners,
    patch_rows,
    patch_cols,
    w_in,
    b_in,
    w_emb,
    w_conv,
    gn_gain,
    gn_bias,
    w_out,
    b_out,
):
    cond = gather_members(coarse_cond, lax.axis_size("member"))
    channels = w_conv.shape[1]
    variables, tile_rows, tile_cols = noisy_state.shape[1:]
    slots = owners.size
    blend = window_weights(PH)[:, None] * window_weights(PW)[None, :]
    blend_cells = jnp.asarray(
        np.broadcast_to(blend[:, :, None], (PH, PW, channels)).astype(np.float32)
    )
    blend_lanes = jnp.asarray(
        np.pad(blend, ((0, 0), (0, tile_cols - PW))).astype(np.float32)
    )
    plan, features = noise_plan(w_emb.shape[1] // 2)
    operands = (
        step_index,
        jnp.asarray(plan),
        jnp.transpose(owners, (0, 2, 1)),
        patch_rows,
        patch_cols,
        b_out,
        w_conv,
        w_emb,
        jnp.asarray(features),
        b_in[None, :],
        noisy_state[0],
        churn_noise[0],
        cond,
        w_in.T,
        land_mask,
        gn_gain[None, :],
        gn_bias[None, :],
        blend_lanes,
        blend_cells,
        w_out,
    )
    f32 = jnp.float32
    result = pl.pallas_call(
        tile_kernel,
        out_shape=jax.ShapeDtypeStruct((variables, tile_rows, tile_cols), f32),
        in_specs=[pl.BlockSpec(memory_space=pltpu.SMEM)]
        + [pl.BlockSpec(memory_space=pltpu.HBM)] * (len(operands) - 1),
        out_specs=pl.BlockSpec(memory_space=pltpu.VMEM),
        scratch_shapes=[pltpu.SMEM(value.shape, value.dtype) for value in operands[1:6]]
        + [pltpu.VMEM(value.shape, value.dtype) for value in operands[6:]]
        + [
            pltpu.SemaphoreType.DMA((len(operands) - 1,)),
            pltpu.SMEM((slots + 1,), jnp.int32),
            pltpu.SMEM((slots + 1,), jnp.int32),
            pltpu.VMEM((K_IN * tile_rows, tile_cols), f32),
            pltpu.VMEM((channels, channels), f32),
            pltpu.VMEM((tile_rows, tile_cols + 2 * LEAD, channels), f32),
            pltpu.VMEM((tile_rows, tile_cols, channels), f32),
            pltpu.VMEM((3, PH // 2 + 1, PW, 2 * channels), jnp.bfloat16),
            pltpu.VMEM((12 * channels, 2 * channels), jnp.bfloat16),
            pltpu.VMEM((PH * PW // 2, 2 * channels), f32),
            pltpu.VMEM((tile_rows, tile_cols), f32),
            pltpu.VMEM((8 * tile_rows, tile_cols), f32),
        ],
        compiler_params=pltpu.CompilerParams(vmem_limit_bytes=67108864),
    )(*operands)
    return result[None]


def solution(mesh):
    return jax.shard_map(
        body,
        mesh=mesh,
        in_specs=(
            P("member", None, "tile", None),
            P("member", None, "tile", None),
            P("member", "tile", None),
            P("tile", None),
            P(),
            P(),
            P(),
            P(),
            P(),
            P(),
            P(),
            P(),
            P(),
            P(),
            P(),
            P(),
        ),
        out_specs=P("member", None, "tile", None),
        check_vma=False,
    )
```

```python
import functools

import jax
import jax.numpy as jnp
import numpy as np
from jax import lax
from jax.experimental import pallas as pl
from jax.experimental.pallas import tpu as pltpu
from jax.sharding import PartitionSpec as P

PH = 32
PW = 32
NSTEPS = 18


SIGMA_DATA = 0.5
GAMMA = 0.25


def noise_plan(half_width):
    index = np.arange(NSTEPS, dtype=np.float64)
    top_root = 800.0 ** (1.0 / 7.0)
    low_root = 0.002 ** (1.0 / 7.0)

    def sigma_at(position):
        return (top_root + position / (NSTEPS - 1) * (low_root - top_root)) ** 7

    sigma_now = sigma_at(index)
    sigma_next = sigma_at(index + 1)
    sigma_hat = (1.0 + GAMMA) * sigma_now
    sigma_sq_sum = sigma_hat * sigma_hat + SIGMA_DATA * SIGMA_DATA
    columns = [
        1.0 / np.sqrt(sigma_sq_sum),
        np.sqrt(GAMMA * (2.0 + GAMMA)) * sigma_now,
        SIGMA_DATA * SIGMA_DATA / sigma_sq_sum,
        SIGMA_DATA * sigma_hat / np.sqrt(sigma_sq_sum),
        (sigma_next - sigma_hat) / sigma_hat,
    ]
    columns += [np.zeros_like(index)] * (8 - len(columns))
    frequency = np.exp(-np.log(10000.0) * np.arange(half_width) / half_width)
    angles = 250.0 * np.log(sigma_hat)[:, None] * frequency[None, :]
    features = np.concatenate([np.cos(angles), np.sin(angles)], axis=1)
    return np.stack(columns, axis=1).reshape(-1).astype(np.float32), features.astype(np.float32)


def window_weights(length):
    position = np.arange(length, dtype=np.float64)
    return 0.3 + 0.7 * np.sin(np.pi * (position + 0.5) / length)


def gather_kernel(axis_size, part_ref, whole_ref, send_sem, recv_sem, local_sem):
    me = lax.axis_index("member")
    depth = part_ref.shape[0]
    barrier = pltpu.get_barrier_semaphore()
    for step in range(1, axis_size):
        pl.semaphore_signal(
            barrier,
            inc=1,
            device_id={"member": lax.rem(me + step, axis_size)},
            device_id_type=pl.DeviceIdType.MESH,
        )
    pl.semaphore_wait(barrier, axis_size - 1)
    own = whole_ref.at[pl.ds(me * depth, depth)]
    copies = []
    for step in range(1, axis_size):
        copy = pltpu.make_async_remote_copy(
            src_ref=part_ref,
            dst_ref=own,
            send_sem=send_sem.at[step - 1],
            recv_sem=recv_sem.at[step - 1],
            device_id={"member": lax.rem(me + step, axis_size)},
            device_id_type=pl.DeviceIdType.MESH,
        )
        copy.start()
        copies.append(copy)
    local = pltpu.make_async_copy(part_ref, own, local_sem)
    local.start()
    local.wait()
    for copy in copies:
        copy.wait()


def gather_members(part, axis_size):
    shape = (part.shape[0] * axis_size,) + part.shape[1:]
    return pl.pallas_call(
        functools.partial(gather_kernel, axis_size),
        out_shape=jax.ShapeDtypeStruct(shape, part.dtype),
        in_specs=[pl.BlockSpec(memory_space=pltpu.HBM)],
        out_specs=pl.BlockSpec(memory_space=pltpu.HBM),
        scratch_shapes=[
            pltpu.SemaphoreType.DMA((axis_size - 1,)),
            pltpu.SemaphoreType.DMA((axis_size - 1,)),
            pltpu.SemaphoreType.DMA,
        ],
        compiler_params=pltpu.CompilerParams(collective_id=0, has_side_effects=True),
    )(part)


LEAD = 8
K_IN = 32


def silu(value):
    half = 0.5 * value
    return half + half * jnp.tanh(half)


def group_sum(value):
    lane = lax.broadcasted_iota(jnp.int32, value.shape, 1)
    width = value.shape[1]
    pair = value + jnp.where(
        lane % 2 == 0, pltpu.roll(value, width - 1, 1), pltpu.roll(value, 1, 1)
    )
    return pair + jnp.where(
        lane % 4 < 2, pltpu.roll(pair, width - 2, 1), pltpu.roll(pair, 2, 1)
    )


def tile_kernel(
    step_index,
    plan_hbm,
    owners_hbm,
    patch_rows_hbm,
    patch_cols_hbm,
    b_out_hbm,
    w_conv_hbm,
    w_emb_hbm,
    features_hbm,
    b_in_hbm,
    noisy_hbm,
    churn_hbm,
    cond_hbm,
    w_in_hbm,
    land_hbm,
    gn_gain_hbm,
    gn_bias_hbm,
    blend_lanes_hbm,
    blend_cells_hbm,
    w_out_hbm,
    out,
    plan,
    owners,
    patch_rows,
    patch_cols,
    b_out,
    w_conv,
    w_emb,
    features,
    b_in,
    noisy,
    churn,
    cond,
    w_in,
    land,
    gn_gain,
    gn_bias,
    blend_lanes,
    blend_cells,
    w_out,
    operand_sem,
    row_list,
    col_list,
    inputs,
    w_square,
    hidden,
    total,
    taps_even,
    taps_odd,
    w_pairs,
    conv_even,
    conv_odd,
    sums,
    weights,
    flat,
):
    pairs = (
        (plan_hbm, plan),
        (owners_hbm, owners),
        (patch_rows_hbm, patch_rows),
        (patch_cols_hbm, patch_cols),
        (b_out_hbm, b_out),
        (w_conv_hbm, w_conv),
        (w_emb_hbm, w_emb),
        (features_hbm, features),
        (b_in_hbm, b_in),
        (noisy_hbm, noisy),
        (churn_hbm, churn),
        (cond_hbm, cond),
        (w_in_hbm, w_in),
        (land_hbm, land),
        (gn_gain_hbm, gn_gain),
        (gn_bias_hbm, gn_bias),
        (blend_lanes_hbm, blend_lanes),
        (blend_cells_hbm, blend_cells.at[1]),
        (w_out_hbm, w_out),
    )
    copies = [
        pltpu.make_async_copy(source, target, operand_sem.at[index])
        for index, (source, target) in enumerate(pairs)
    ]
    for copy in copies:
        copy.start()
    self_tile = lax.axis_index("tile")
    channels = w_conv.shape[1]
    variables, tile_rows, tile_cols = noisy.shape
    cond_channels = cond.shape[0]

    def clear_row(row, carry):
        total[row] = jnp.zeros((tile_cols, channels), jnp.float32)
        return carry

    lax.fori_loop(0, tile_rows, clear_row, 0, unroll=4)
    blend_cells[0] = jnp.zeros(blend_cells.shape[1:], jnp.float32)
    copies[5].wait()
    zero_block = jnp.zeros((channels, channels), jnp.bfloat16)
    for col in range(3):
        tap = [w_conv[3 * a + col].astype(jnp.float32).T.astype(jnp.bfloat16) for a in range(3)]
        blocks = (
            ((tap[0], zero_block), (tap[1], tap[0])),
            ((tap[2], tap[1]), (zero_block, tap[2])),
        )
        for half in range(2):
            start = (2 * col + half) * 2 * channels
            for k in range(2):
                for o in range(2):
                    w_pairs[
                        start + k * channels : start + (k + 1) * channels,
                        o * channels : (o + 1) * channels,
                    ] = blocks[half][k][o]
        for taps in (taps_even, taps_odd):
            taps[col, 0, :, 0:channels] = jnp.zeros((PW, channels), jnp.bfloat16)
            taps[col, PH // 2, :, channels : 2 * channels] = jnp.zeros(
                (PW, channels), jnp.bfloat16
            )
    weights[...] = jnp.zeros_like(weights)
    for index, copy in enumerate(copies[:13]):
        if index != 5:
            copy.wait()
    step = step_index[0]
    scale_in = plan[8 * step]
    churn_scale = plan[8 * step + 1]
    scale_skip = plan[8 * step + 2]
    scale_out = plan[8 * step + 3]
    step_ratio = plan[8 * step + 4]
    feature = jnp.broadcast_to(features[pl.ds(step, 1), :], (8, features.shape[1]))
    embedding = lax.dot_general(
        feature,
        w_emb[...],
        (((1,), (1,)), ((), ())),
        precision=lax.Precision.HIGHEST,
        preferred_element_type=jnp.float32,
    )
    bias = b_in[...] + embedding[0:1]
    slots = patch_rows.shape[1]
    scanned = patch_rows.shape[0] * slots // tile_rows
    assert scanned * tile_rows == patch_rows.shape[0] * slots

    for channel in range(cond_channels):
        inputs[channel * tile_rows : (channel + 1) * tile_rows, :] = cond[channel].astype(
            jnp.float32
        )
    for variable in range(variables):
        start = (cond_channels + variable) * tile_rows
        x_hat = noisy[variable] + churn_scale * churn[variable]
        inputs[start : start + tile_rows, :] = (
            (scale_in * x_hat).astype(jnp.bfloat16).astype(jnp.float32)
        )
    used = cond_channels + variables
    inputs[used * tile_rows :, :] = jnp.zeros(
        ((K_IN - used) * tile_rows, tile_cols), jnp.float32
    )
    w_square[...] = jnp.zeros_like(w_square)
    w_square[0:used, :] = w_in[...].astype(jnp.float32)
    w_first = w_square[0:K_IN].astype(jnp.bfloat16)

    def hidden_row(row, count):
        cells = inputs[pl.ds(row, K_IN, stride=tile_rows), :].T.astype(jnp.bfloat16)
        pre_act = jnp.dot(cells, w_first, preferred_element_type=jnp.float32) + bias
        hidden[row, LEAD : LEAD + tile_cols, :] = (
            silu(pre_act).astype(jnp.bfloat16).astype(jnp.float32)
        )
        for entry in range(scanned):
            worker = (row * scanned + entry) // slots
            slot = (row * scanned + entry) % slots
            row_list[count] = patch_rows[worker, slot]
            col_list[count] = patch_cols[worker, slot]
            count = count + (owners[worker, 0, slot] == self_tile).astype(jnp.int32)
        return count

    count = lax.fori_loop(0, tile_rows, hidden_row, jnp.int32(0), unroll=8)
    for copy in copies[13:]:
        copy.wait()

    gain = jnp.concatenate([gn_gain[...], gn_gain[...]], axis=1)
    shift = jnp.concatenate([gn_bias[...], gn_bias[...]], axis=1)
    lanes = blend_lanes[...]
    cell_count = PH * PW
    inverse = 1.0 / (4 * cell_count)
    position = lax.broadcasted_iota(jnp.int32, (PW, channels), 0)

    def spread(value):
        value = group_sum(value[:, 0:channels] + value[:, channels : 2 * channels])
        return jnp.concatenate([value, value], axis=1)

    def convolve(slot, taps, conv, parity):
        slot = jnp.minimum(slot, jnp.maximum(count - 1, 0))
        row_start = row_list[slot]
        col_start = col_list[slot]
        for i in range(PH):
            pair = (i + 1) // 2
            lane = 0 if i % 2 else channels
            for col in range(3):
                piece = hidden[row_start + i, pl.ds(col_start + (LEAD - 1 + col), PW), :]
                if col == 0:
                    piece = jnp.where(position == 0, 0.0, piece)
                if col == 2:
                    piece = jnp.where(position == PW - 1, 0.0, piece)
                taps[col, pair, :, lane : lane + channels] = piece.astype(jnp.bfloat16)
        half_cells = cell_count // 2
        left = jnp.concatenate(
            [
                taps[col, half : half + PH // 2].reshape(half_cells, 2 * channels)
                for col in range(3)
                for half in range(2)
            ],
            axis=1,
        )
        convolved = jnp.dot(left, w_pairs[...], preferred_element_type=jnp.float32)
        conv[...] = convolved
        sums[parity : parity + 1, :] = jnp.sum(convolved, axis=0, keepdims=True)

    def finish(slot, conv, parity):
        live = (slot < count).astype(jnp.int32)
        slot = jnp.minimum(slot, count - 1)
        row_start = row_list[slot]
        col_start = col_list[slot]
        mean = spread(sums[parity : parity + 1, :]) * inverse
        squares = jnp.zeros((8, 2 * channels), jnp.float32)
        for t in range(PH // 2):
            centred = conv[t * PW : (t + 1) * PW, :] - mean
            centred = (centred * centred).reshape(PW // 8, 8, 2 * channels)
            squares = squares + jnp.sum(centred, axis=0)
        var = spread(jnp.sum(squares, axis=0, keepdims=True)) * inverse
        scale = lax.rsqrt(var + 1e-06) * gain
        weights[pl.ds(row_start, PH), :] += pltpu.roll(
            lanes * live.astype(jnp.float32), col_start, 1
        )
        for t in range(PH // 2):
            normed = (conv[t * PW : (t + 1) * PW, :] - mean) * scale + shift
            active = silu(normed)
            for o in range(2):
                i = 2 * t + o
                own = hidden[row_start + i, pl.ds(col_start + LEAD, PW), :]
                residual = (
                    (own + active[:, o * channels : (o + 1) * channels])
                    .astype(jnp.bfloat16)
                    .astype(jnp.float32)
                )
                total[row_start + i, pl.ds(col_start, PW), :] += residual * blend_cells[live, i]

    convolve(0, taps_even, conv_even, 0)

    def two_patches(turn, carry):
        slot = 2 * turn
        convolve(slot + 1, taps_odd, conv_odd, 1)
        finish(slot, conv_even, 0)
        convolve(slot + 2, taps_even, conv_even, 0)
        finish(slot + 1, conv_odd, 1)
        return carry

    lax.fori_loop(0, (count + 1) // 2, two_patches, 0)

    w_square[0:16, :] = jnp.zeros((16, channels), jnp.float32)
    w_square[0:variables, :] = w_out[...].astype(jnp.float32)
    w_last = w_square[0:16, :].astype(jnp.bfloat16)
    w_last = jnp.concatenate([w_last, w_last], axis=1)

    def project(block, carry):
        value = total[pl.ds(block * 8, 8)].reshape(8 * tile_cols, channels)
        high = value.astype(jnp.bfloat16)
        low = (value - high.astype(jnp.float32)).astype(jnp.bfloat16)
        result = lax.dot_general(
            w_last,
            jnp.concatenate([high, low], axis=1),
            (((1,), (1,)), ((), ())),
            preferred_element_type=jnp.float32,
        )
        for j in range(8):
            flat[pl.ds(pl.multiple_of(block * 64, 64) + j * 8, 8), :] = result[
                0:8, j * tile_cols : (j + 1) * tile_cols
            ]
        return carry

    lax.fori_loop(0, tile_rows // 8, project, 0)

    cover = weights[...]
    land_value = land[...].astype(jnp.float32) / jnp.maximum(cover, 0.25)
    for variable in range(variables):
        x_hat = noisy[variable] + churn_scale * churn[variable]
        accumulated = flat[pl.ds(variable, tile_rows, stride=8), :] + b_out[variable] * cover
        denoised = land_value * (cover * scale_skip * x_hat + scale_out * accumulated)
        out[variable] = x_hat + step_ratio * (x_hat - denoised)


def body(
    noisy_state,
    churn_noise,
    coarse_cond,
    land_mask,
    step_index,
    owners,
    patch_rows,
    patch_cols,
    w_in,
    b_in,
    w_emb,
    w_conv,
    gn_gain,
    gn_bias,
    w_out,
    b_out,
):
    cond = gather_members(coarse_cond, lax.axis_size("member"))
    channels = w_conv.shape[1]
    variables, tile_rows, tile_cols = noisy_state.shape[1:]
    slots = owners.size
    blend = window_weights(PH)[:, None] * window_weights(PW)[None, :]
    blend_cells = jnp.asarray(
        np.broadcast_to(blend[:, :, None], (PH, PW, channels)).astype(np.float32)
    )
    blend_lanes = jnp.asarray(
        np.pad(blend, ((0, 0), (0, tile_cols - PW))).astype(np.float32)
    )
    plan, features = noise_plan(w_emb.shape[1] // 2)
    operands = (
        step_index,
        jnp.asarray(plan),
        jnp.transpose(owners, (0, 2, 1)),
        patch_rows,
        patch_cols,
        b_out,
        w_conv,
        w_emb,
        jnp.asarray(features),
        b_in[None, :],
        noisy_state[0],
        churn_noise[0],
        cond,
        w_in.T,
        land_mask,
        gn_gain[None, :],
        gn_bias[None, :],
        blend_lanes,
        blend_cells,
        w_out,
    )
    f32 = jnp.float32
    result = pl.pallas_call(
        tile_kernel,
        out_shape=jax.ShapeDtypeStruct((variables, tile_rows, tile_cols), f32),
        in_specs=[pl.BlockSpec(memory_space=pltpu.SMEM)]
        + [pl.BlockSpec(memory_space=pltpu.HBM)] * (len(operands) - 1),
        out_specs=pl.BlockSpec(memory_space=pltpu.VMEM),
        scratch_shapes=[pltpu.SMEM(value.shape, value.dtype) for value in operands[1:6]]
        + [pltpu.VMEM(value.shape, value.dtype) for value in operands[6:-2]]
        + [pltpu.VMEM((2,) + blend_cells.shape, f32), pltpu.VMEM(w_out.shape, w_out.dtype)]
        + [
            pltpu.SemaphoreType.DMA((len(operands) - 1,)),
            pltpu.SMEM((slots + 1,), jnp.int32),
            pltpu.SMEM((slots + 1,), jnp.int32),
            pltpu.VMEM((K_IN * tile_rows, tile_cols), f32),
            pltpu.VMEM((channels, channels), f32),
            pltpu.VMEM((tile_rows, tile_cols + 2 * LEAD, channels), f32),
            pltpu.VMEM((tile_rows, tile_cols, channels), f32),
            pltpu.VMEM((3, PH // 2 + 1, PW, 2 * channels), jnp.bfloat16),
            pltpu.VMEM((3, PH // 2 + 1, PW, 2 * channels), jnp.bfloat16),
            pltpu.VMEM((12 * channels, 2 * channels), jnp.bfloat16),
            pltpu.VMEM((PH * PW // 2, 2 * channels), f32),
            pltpu.VMEM((PH * PW // 2, 2 * channels), f32),
            pltpu.VMEM((2, 2 * channels), f32),
            pltpu.VMEM((tile_rows, tile_cols), f32),
            pltpu.VMEM((8 * tile_rows, tile_cols), f32),
        ],
        compiler_params=pltpu.CompilerParams(vmem_limit_bytes=67108864),
    )(*operands)
    return result[None]


def solution(mesh):
    return jax.shard_map(
        body,
        mesh=mesh,
        in_specs=(
            P("member", None, "tile", None),
            P("member", None, "tile", None),
            P("member", "tile", None),
            P("tile", None),
            P(),
            P(),
            P(),
            P(),
            P(),
            P(),
            P(),
            P(),
            P(),
            P(),
            P(),
            P(),
        ),
        out_specs=P("member", None, "tile", None),
        check_vma=False,
    )
```

```python
import functools

import jax
import jax.numpy as jnp
import numpy as np
from jax import lax
from jax.experimental import pallas as pl
from jax.experimental.pallas import tpu as pltpu
from jax.sharding import PartitionSpec as P

PH = 32
PW = 32
NSTEPS = 18


SIGMA_DATA = 0.5
GAMMA = 0.25


def noise_plan(half_width):
    index = np.arange(NSTEPS, dtype=np.float64)
    top_root = 800.0 ** (1.0 / 7.0)
    low_root = 0.002 ** (1.0 / 7.0)

    def sigma_at(position):
        return (top_root + position / (NSTEPS - 1) * (low_root - top_root)) ** 7

    sigma_now = sigma_at(index)
    sigma_next = sigma_at(index + 1)
    sigma_hat = (1.0 + GAMMA) * sigma_now
    sigma_sq_sum = sigma_hat * sigma_hat + SIGMA_DATA * SIGMA_DATA
    columns = [
        1.0 / np.sqrt(sigma_sq_sum),
        np.sqrt(GAMMA * (2.0 + GAMMA)) * sigma_now,
        SIGMA_DATA * SIGMA_DATA / sigma_sq_sum,
        SIGMA_DATA * sigma_hat / np.sqrt(sigma_sq_sum),
        (sigma_next - sigma_hat) / sigma_hat,
    ]
    columns += [np.zeros_like(index)] * (8 - len(columns))
    frequency = np.exp(-np.log(10000.0) * np.arange(half_width) / half_width)
    angles = 250.0 * np.log(sigma_hat)[:, None] * frequency[None, :]
    features = np.concatenate([np.cos(angles), np.sin(angles)], axis=1)
    return np.stack(columns, axis=1).reshape(-1).astype(np.float32), features.astype(np.float32)


def window_weights(length):
    position = np.arange(length, dtype=np.float64)
    return 0.3 + 0.7 * np.sin(np.pi * (position + 0.5) / length)


def gather_kernel(axis_size, part_ref, whole_ref, send_sem, recv_sem, local_sem):
    me = lax.axis_index("member")
    depth = part_ref.shape[0]
    barrier = pltpu.get_barrier_semaphore()
    for step in range(1, axis_size):
        pl.semaphore_signal(
            barrier,
            inc=1,
            device_id={"member": lax.rem(me + step, axis_size)},
            device_id_type=pl.DeviceIdType.MESH,
        )
    pl.semaphore_wait(barrier, axis_size - 1)
    own = whole_ref.at[pl.ds(me * depth, depth)]
    copies = []
    for step in range(1, axis_size):
        copy = pltpu.make_async_remote_copy(
            src_ref=part_ref,
            dst_ref=own,
            send_sem=send_sem.at[step - 1],
            recv_sem=recv_sem.at[step - 1],
            device_id={"member": lax.rem(me + step, axis_size)},
            device_id_type=pl.DeviceIdType.MESH,
        )
        copy.start()
        copies.append(copy)
    local = pltpu.make_async_copy(part_ref, own, local_sem)
    local.start()
    local.wait()
    for copy in copies:
        copy.wait()


def gather_members(part, axis_size):
    shape = (part.shape[0] * axis_size,) + part.shape[1:]
    return pl.pallas_call(
        functools.partial(gather_kernel, axis_size),
        out_shape=jax.ShapeDtypeStruct(shape, part.dtype),
        in_specs=[pl.BlockSpec(memory_space=pltpu.HBM)],
        out_specs=pl.BlockSpec(memory_space=pltpu.HBM),
        scratch_shapes=[
            pltpu.SemaphoreType.DMA((axis_size - 1,)),
            pltpu.SemaphoreType.DMA((axis_size - 1,)),
            pltpu.SemaphoreType.DMA,
        ],
        compiler_params=pltpu.CompilerParams(collective_id=0, has_side_effects=True),
    )(part)


LEAD = 8
K_IN = 32


def silu(value):
    half = 0.5 * value
    return half + half * jnp.tanh(half)


def group_sum(value):
    lane = lax.broadcasted_iota(jnp.int32, value.shape, 1)
    width = value.shape[1]
    pair = value + jnp.where(
        lane % 2 == 0, pltpu.roll(value, width - 1, 1), pltpu.roll(value, 1, 1)
    )
    return pair + jnp.where(
        lane % 4 < 2, pltpu.roll(pair, width - 2, 1), pltpu.roll(pair, 2, 1)
    )


def tile_kernel(
    step_index,
    plan_hbm,
    owners_hbm,
    patch_rows_hbm,
    patch_cols_hbm,
    b_out_hbm,
    w_conv_hbm,
    w_emb_hbm,
    features_hbm,
    b_in_hbm,
    noisy_hbm,
    churn_hbm,
    cond_hbm,
    w_in_hbm,
    land_hbm,
    gn_gain_hbm,
    gn_bias_hbm,
    blend_lanes_hbm,
    blend_cells_hbm,
    w_out_hbm,
    out,
    plan,
    owners,
    patch_rows,
    patch_cols,
    b_out,
    w_conv,
    w_emb,
    features,
    b_in,
    noisy,
    churn,
    cond,
    w_in,
    land,
    gn_gain,
    gn_bias,
    blend_lanes,
    blend_cells,
    w_out,
    operand_sem,
    row_list,
    col_list,
    inputs,
    w_square,
    hidden,
    total,
    taps_even,
    taps_odd,
    w_pairs,
    conv_even,
    conv_odd,
    sums,
    weights,
    flat,
):
    pairs = (
        (plan_hbm, plan),
        (owners_hbm, owners),
        (patch_rows_hbm, patch_rows),
        (patch_cols_hbm, patch_cols),
        (b_out_hbm, b_out),
        (w_conv_hbm, w_conv),
        (w_emb_hbm, w_emb),
        (features_hbm, features),
        (b_in_hbm, b_in),
        (noisy_hbm, noisy),
        (churn_hbm, churn),
        (cond_hbm, cond),
        (w_in_hbm, w_in),
        (land_hbm, land),
        (gn_gain_hbm, gn_gain),
        (gn_bias_hbm, gn_bias),
        (blend_lanes_hbm, blend_lanes),
        (blend_cells_hbm, blend_cells.at[1]),
        (w_out_hbm, w_out),
    )
    copies = [
        pltpu.make_async_copy(source, target, operand_sem.at[index])
        for index, (source, target) in enumerate(pairs)
    ]
    for copy in copies:
        copy.start()
    self_tile = lax.axis_index("tile")
    channels = w_conv.shape[1]
    variables, tile_rows, tile_cols = noisy.shape
    cond_channels = cond.shape[0]

    def clear_row(row, carry):
        total[row] = jnp.zeros((tile_cols, channels), jnp.float32)
        return carry

    lax.fori_loop(0, tile_rows, clear_row, 0, unroll=4)
    blend_cells[0] = jnp.zeros(blend_cells.shape[1:], jnp.float32)
    copies[5].wait()
    zero_block = jnp.zeros((channels, channels), jnp.bfloat16)
    for col in range(3):
        tap = [w_conv[3 * a + col].astype(jnp.float32).T.astype(jnp.bfloat16) for a in range(3)]
        blocks = (
            ((tap[0], zero_block), (tap[1], tap[0])),
            ((tap[2], tap[1]), (zero_block, tap[2])),
        )
        for half in range(2):
            start = (2 * col + half) * 2 * channels
            for k in range(2):
                for o in range(2):
                    w_pairs[
                        start + k * channels : start + (k + 1) * channels,
                        o * channels : (o + 1) * channels,
                    ] = blocks[half][k][o]
        for taps in (taps_even, taps_odd):
            taps[col, 0, :, 0:channels] = jnp.zeros((PW, channels), jnp.bfloat16)
            taps[col, PH // 2, :, channels : 2 * channels] = jnp.zeros(
                (PW, channels), jnp.bfloat16
            )
    weights[...] = jnp.zeros_like(weights)
    for index, copy in enumerate(copies[:13]):
        if index != 5:
            copy.wait()
    step = step_index[0]
    scale_in = plan[8 * step]
    churn_scale = plan[8 * step + 1]
    scale_skip = plan[8 * step + 2]
    scale_out = plan[8 * step + 3]
    step_ratio = plan[8 * step + 4]
    feature = jnp.broadcast_to(features[pl.ds(step, 1), :], (8, features.shape[1]))
    embedding = lax.dot_general(
        feature,
        w_emb[...],
        (((1,), (1,)), ((), ())),
        precision=lax.Precision.HIGHEST,
        preferred_element_type=jnp.float32,
    )
    bias = b_in[...] + embedding[0:1]
    slots = patch_rows.shape[1]
    scanned = patch_rows.shape[0] * slots // tile_rows
    assert scanned * tile_rows == patch_rows.shape[0] * slots

    for channel in range(cond_channels):
        inputs[channel * tile_rows : (channel + 1) * tile_rows, :] = cond[channel].astype(
            jnp.float32
        )
    for variable in range(variables):
        start = (cond_channels + variable) * tile_rows
        x_hat = noisy[variable] + churn_scale * churn[variable]
        inputs[start : start + tile_rows, :] = (
            (scale_in * x_hat).astype(jnp.bfloat16).astype(jnp.float32)
        )
    used = cond_channels + variables
    inputs[used * tile_rows :, :] = jnp.zeros(
        ((K_IN - used) * tile_rows, tile_cols), jnp.float32
    )
    w_square[...] = jnp.zeros_like(w_square)
    w_square[0:used, :] = w_in[...].astype(jnp.float32)
    w_first = w_square[0:K_IN].astype(jnp.bfloat16)

    def hidden_row(row, count):
        cells = inputs[pl.ds(row, K_IN, stride=tile_rows), :].T.astype(jnp.bfloat16)
        pre_act = jnp.dot(cells, w_first, preferred_element_type=jnp.float32) + bias
        hidden[row, LEAD : LEAD + tile_cols, :] = (
            silu(pre_act).astype(jnp.bfloat16).astype(jnp.float32)
        )
        for entry in range(scanned):
            worker = (row * scanned + entry) // slots
            slot = (row * scanned + entry) % slots
            row_list[count] = patch_rows[worker, slot]
            col_list[count] = patch_cols[worker, slot]
            count = count + (owners[worker, 0, slot] == self_tile).astype(jnp.int32)
        return count

    count = lax.fori_loop(0, tile_rows, hidden_row, jnp.int32(0), unroll=8)
    for copy in copies[13:]:
        copy.wait()

    gain = jnp.concatenate([gn_gain[...], gn_gain[...]], axis=1)
    shift = jnp.concatenate([gn_bias[...], gn_bias[...]], axis=1)
    lanes = blend_lanes[...]
    cell_count = PH * PW
    inverse = 1.0 / (4 * cell_count)
    position = lax.broadcasted_iota(jnp.int32, (8, channels), 0)

    def spread(value):
        value = group_sum(value[:, 0:channels] + value[:, channels : 2 * channels])
        return jnp.concatenate([value, value], axis=1)

    def convolve(slot, taps, conv, parity):
        slot = jnp.minimum(slot, jnp.maximum(count - 1, 0))
        row_start = row_list[slot]
        col_start = col_list[slot]
        for i in range(PH):
            pair = (i + 1) // 2
            lane = 0 if i % 2 else channels
            for col in range(3):
                piece = hidden[row_start + i, pl.ds(col_start + (LEAD - 1 + col), PW), :]
                if col == 0:
                    edge = jnp.where(position == 0, 0.0, piece[0:8])
                    piece = jnp.concatenate([edge, piece[8:PW]], axis=0)
                if col == 2:
                    edge = jnp.where(position == 7, 0.0, piece[PW - 8 : PW])
                    piece = jnp.concatenate([piece[0 : PW - 8], edge], axis=0)
                taps[col, pair, :, lane : lane + channels] = piece.astype(jnp.bfloat16)
        half_cells = cell_count // 2
        left = jnp.concatenate(
            [
                taps[col, half : half + PH // 2].reshape(half_cells, 2 * channels)
                for col in range(3)
                for half in range(2)
            ],
            axis=1,
        )
        convolved = jnp.dot(left, w_pairs[...], preferred_element_type=jnp.float32)
        conv[...] = convolved
        sums[parity : parity + 1, :] = jnp.sum(convolved, axis=0, keepdims=True)

    def finish(slot, conv, parity):
        live = (slot < count).astype(jnp.int32)
        slot = jnp.minimum(slot, count - 1)
        row_start = row_list[slot]
        col_start = col_list[slot]
        mean = spread(sums[parity : parity + 1, :]) * inverse
        squares = jnp.zeros((8, 2 * channels), jnp.float32)
        for t in range(PH // 2):
            centred = conv[t * PW : (t + 1) * PW, :] - mean
            centred = (centred * centred).reshape(PW // 8, 8, 2 * channels)
            squares = squares + jnp.sum(centred, axis=0)
        var = spread(jnp.sum(squares, axis=0, keepdims=True)) * inverse
        scale = lax.rsqrt(var + 1e-06) * gain
        weights[pl.ds(row_start, PH), :] += pltpu.roll(
            lanes * live.astype(jnp.float32), col_start, 1
        )
        for quad in range(PH // 4):
            parts = []
            for t in (2 * quad, 2 * quad + 1):
                normed = (conv[t * PW : (t + 1) * PW, :] - mean) * scale + shift
                active = silu(normed)
                parts += [active[:, 0:channels], active[:, channels : 2 * channels]]
            cells = pl.ds(row_start + 4 * quad, 4)
            own = hidden[cells, pl.ds(col_start + LEAD, PW), :]
            residual = (own + jnp.stack(parts)).astype(jnp.bfloat16).astype(jnp.float32)
            total[cells, pl.ds(col_start, PW), :] += (
                residual * blend_cells[live, 4 * quad : 4 * quad + 4]
            )

    convolve(0, taps_even, conv_even, 0)

    def two_patches(turn, carry):
        slot = 2 * turn
        finish(slot, conv_even, 0)
        convolve(slot + 1, taps_odd, conv_odd, 1)
        finish(slot + 1, conv_odd, 1)
        convolve(slot + 2, taps_even, conv_even, 0)
        return carry

    lax.fori_loop(0, (count + 1) // 2, two_patches, 0)

    w_square[0:16, :] = jnp.zeros((16, channels), jnp.float32)
    w_square[0:variables, :] = w_out[...].astype(jnp.float32)
    w_last = w_square[0:16, :].astype(jnp.bfloat16)
    w_last = jnp.concatenate([w_last, w_last], axis=1)

    def project(block, carry):
        value = total[pl.ds(block * 8, 8)].reshape(8 * tile_cols, channels)
        high = value.astype(jnp.bfloat16)
        low = (value - high.astype(jnp.float32)).astype(jnp.bfloat16)
        result = lax.dot_general(
            w_last,
            jnp.concatenate([high, low], axis=1),
            (((1,), (1,)), ((), ())),
            preferred_element_type=jnp.float32,
        )
        for j in range(8):
            flat[pl.ds(pl.multiple_of(block * 64, 64) + j * 8, 8), :] = result[
                0:8, j * tile_cols : (j + 1) * tile_cols
            ]
        return carry

    lax.fori_loop(0, tile_rows // 8, project, 0, unroll=2)

    cover = weights[...]
    land_value = land[...].astype(jnp.float32) / jnp.maximum(cover, 0.25)
    for variable in range(variables):
        x_hat = noisy[variable] + churn_scale * churn[variable]
        accumulated = flat[pl.ds(variable, tile_rows, stride=8), :] + b_out[variable] * cover
        denoised = land_value * (cover * scale_skip * x_hat + scale_out * accumulated)
        out[variable] = x_hat + step_ratio * (x_hat - denoised)


def body(
    noisy_state,
    churn_noise,
    coarse_cond,
    land_mask,
    step_index,
    owners,
    patch_rows,
    patch_cols,
    w_in,
    b_in,
    w_emb,
    w_conv,
    gn_gain,
    gn_bias,
    w_out,
    b_out,
):
    cond = gather_members(coarse_cond, lax.axis_size("member"))
    channels = w_conv.shape[1]
    variables, tile_rows, tile_cols = noisy_state.shape[1:]
    slots = owners.size
    blend = window_weights(PH)[:, None] * window_weights(PW)[None, :]
    blend_cells = jnp.asarray(
        np.broadcast_to(blend[:, :, None], (PH, PW, channels)).astype(np.float32)
    )
    blend_lanes = jnp.asarray(
        np.pad(blend, ((0, 0), (0, tile_cols - PW))).astype(np.float32)
    )
    plan, features = noise_plan(w_emb.shape[1] // 2)
    operands = (
        step_index,
        jnp.asarray(plan),
        jnp.transpose(owners, (0, 2, 1)),
        patch_rows,
        patch_cols,
        b_out,
        w_conv,
        w_emb,
        jnp.asarray(features),
        b_in[None, :],
        noisy_state[0],
        churn_noise[0],
        cond,
        w_in.T,
        land_mask,
        gn_gain[None, :],
        gn_bias[None, :],
        blend_lanes,
        blend_cells,
        w_out,
    )
    f32 = jnp.float32
    result = pl.pallas_call(
        tile_kernel,
        out_shape=jax.ShapeDtypeStruct((variables, tile_rows, tile_cols), f32),
        in_specs=[pl.BlockSpec(memory_space=pltpu.SMEM)]
        + [pl.BlockSpec(memory_space=pltpu.HBM)] * (len(operands) - 1),
        out_specs=pl.BlockSpec(memory_space=pltpu.VMEM),
        scratch_shapes=[pltpu.SMEM(value.shape, value.dtype) for value in operands[1:6]]
        + [pltpu.VMEM(value.shape, value.dtype) for value in operands[6:-2]]
        + [pltpu.VMEM((2,) + blend_cells.shape, f32), pltpu.VMEM(w_out.shape, w_out.dtype)]
        + [
            pltpu.SemaphoreType.DMA((len(operands) - 1,)),
            pltpu.SMEM((slots + 1,), jnp.int32),
            pltpu.SMEM((slots + 1,), jnp.int32),
            pltpu.VMEM((K_IN * tile_rows, tile_cols), f32),
            pltpu.VMEM((channels, channels), f32),
            pltpu.VMEM((tile_rows, tile_cols + 2 * LEAD, channels), f32),
            pltpu.VMEM((tile_rows, tile_cols, channels), f32),
            pltpu.VMEM((3, PH // 2 + 1, PW, 2 * channels), jnp.bfloat16),
            pltpu.VMEM((3, PH // 2 + 1, PW, 2 * channels), jnp.bfloat16),
            pltpu.VMEM((12 * channels, 2 * channels), jnp.bfloat16),
            pltpu.VMEM((PH * PW // 2, 2 * channels), f32),
            pltpu.VMEM((PH * PW // 2, 2 * channels), f32),
            pltpu.VMEM((2, 2 * channels), f32),
            pltpu.VMEM((tile_rows, tile_cols), f32),
            pltpu.VMEM((8 * tile_rows, tile_cols), f32),
        ],
        compiler_params=pltpu.CompilerParams(vmem_limit_bytes=67108864),
    )(*operands)
    return result[None]


def solution(mesh):
    return jax.shard_map(
        body,
        mesh=mesh,
        in_specs=(
            P("member", None, "tile", None),
            P("member", None, "tile", None),
            P("member", "tile", None),
            P("tile", None),
            P(),
            P(),
            P(),
            P(),
            P(),
            P(),
            P(),
            P(),
            P(),
            P(),
            P(),
            P(),
        ),
        out_specs=P("member", None, "tile", None),
        check_vma=False,
    )
```
